256 devices in a mesh: dp: 16 (over y, z_hi, core), seq: 16 (over z_lo, x).
Axes of the slice: x: 4, y: 4, z: 8 (z_hi: 2, z_lo: 4; z = z_hi * 4 + z_lo), core: 2. Of those that a mesh axis runs over, the one named last changes fastest.
Arguments:
- query_nope: bfloat16 [32768, 64, 128], P(('dp', 'seq')), may hold values from -6 to 6
- query_rope: bfloat16 [32768, 4096], P(('dp', 'seq')), may hold values from -8 to 8
- out_grad: bfloat16 [32768, 64, 128], P(('dp', 'seq')), may hold values from -6 to 6
- latent_rows: bfloat16 [32768, 576], P(('dp', 'seq')), may hold values from -6 to 6
- prompt_latent: bfloat16 [16, 128, 576], P('dp', 'seq'), may hold values from -8 to 8
- key_weight: bfloat16 [64, 128, 512], P('seq'), may hold values from -0.5 to 0.5
- value_weight: bfloat16 [64, 128, 512], P('seq'), may hold values from -0.25 to 0.25
- prompt_of: int32 [16, 16], replicated, may hold values from 0 to 15
- prompt_len: int32 [16], replicated, may hold values from 32 to 128, as said below
- response_ids: int32 [256, 128], P(('dp', 'seq')), may hold values from 0 to 3, never falling along the last dimension, each value on 1 to 64 neighbouring positions
Outputs:
- grad_nope: bfloat16 [32768, 64, 128], P(('dp', 'seq'))
- grad_rope: bfloat16 [32768, 4096], P(('dp', 'seq'))
- grad_latent: bfloat16 [32768, 576], P(('dp', 'seq'))
- grad_prompt: float32 [16, 128, 576], P('dp', 'seq')
The draws below stay inside these ranges and needn't reach their ends.
Inputs may be any that keep to these rules, and one draw needn't show every extreme that they name: `prompt_len`: some prompt has exactly 128 live rows in every draw.
All inputs are finite; a program needn't handle non-finite values.
Results may differ from the reference program's by a relative error of at most 0.015.
Values may be sent and summed in bfloat16 or wider, within the bound.
No kernel may reach another device: no remote copies, remote signals or barrier semaphores. Data moves between devices by JAX's collectives and lax.ppermute only.
A program may use at most 128 MiB of HBM per device.

```python
import math
import jax
import jax.numpy as jnp
import numpy as np
from jax import lax

HEADS = 64
NOPE = 128
ROPE = 64
LATENT = 512
KV_WIDTH = 576
TOK_DEV = 128
PROMPT = 128
PROMPTS = 16
TOKENS = 32768
N_DP = 16
N_SEQ = 16


def draw_query_rope(key, part):
    key = jax.random.fold_in(key, 11)
    base = jnp.clip(jax.random.normal(key, (TOKENS, HEADS, ROPE), jnp.float32), -6.0, 6.0)
    return base.reshape(TOKENS, HEADS * ROPE).astype(jnp.bfloat16)


def draw_prompt_latent(key, part):
    key = jax.random.fold_in(key, 12)
    base = jnp.clip(jax.random.normal(key, (PROMPTS, PROMPT, KV_WIDTH), jnp.float32), -6.0, 6.0)
    return base.astype(jnp.bfloat16)


def draw_prompt_len(key, part):
    key = jax.random.fold_in(key, 13)
    first_key, second_key = jax.random.split(key)
    sizes_drawn = jax.random.randint(first_key, (PROMPTS,), PROMPT // 4, PROMPT + 1)
    spot = jax.random.randint(second_key, (), 0, PROMPTS)
    return jnp.where(jnp.arange(PROMPTS) == spot, PROMPT, sizes_drawn).astype(jnp.int32)


def plant(entries, own_key, least, largest):
    place = [jax.random.randint(jax.random.fold_in(own_key, axis), (), 0, length) for axis, length in enumerate(entries.shape)]
    longest = entries.shape.index(max(entries.shape))
    beside = place[:longest] + [(place[longest] + 1) % entries.shape[longest]] + place[longest + 1:]
    return entries.at[tuple(place)].set(least).at[tuple(beside)].set(largest)


def block_scale(stream_key, shape, pieces, least, top_value):
    level, own = 1.0, jax.random.fold_in(stream_key, 6)
    for axis_at, blocks in pieces:
        heights = jnp.exp(jax.random.uniform(jax.random.fold_in(own, axis_at), (blocks,), jnp.float32, least / len(pieces), top_value / len(pieces)))
        level = level * jnp.repeat(heights, shape[axis_at] // blocks).reshape([-1 if axis == axis_at else 1 for axis in range(len(shape))])
    return level


def profile(number_of, total, bound, skew):
    weights = [(1 << 20) // math.isqrt(rank ** skew) + 1 for rank in range(2, number_of + 1)]
    rest, given = total - bound - (number_of - 1), [1] * (number_of - 1)
    while rest > 0:
        candidates = [i for i in range(number_of - 1) if given[i] < bound]
        mass, budget = sum([weights[i] for i in candidates]), rest
        for i in candidates:
            more = min(bound - given[i], max(1, budget * weights[i] // mass), rest)
            given[i] = given[i] + more
            rest = rest - more
    return np.array([bound] + given)


def uneven_parts(rng, amount, total, most, slope):
    if amount == 2:
        one = jax.random.randint(rng, (), max(1, total - most), min(most, total - 1) + 1)
        return jnp.stack([one, total - one])
    tallies = jnp.asarray(profile(amount, total, most, slope), jnp.int32)
    pairs = (amount - 1) // 2
    source_of, receiver = tallies[1:1 + 2 * pairs:2], tallies[2:2 + 2 * pairs:2]
    room = jnp.minimum(source_of - 1, most - receiver)
    moved = jax.random.randint(jax.random.fold_in(rng, 1), (pairs,), 0, 1 << 20) % (room + 1)
    tallies = tallies.at[1:1 + 2 * pairs:2].set(source_of - moved).at[2:2 + 2 * pairs:2].set(receiver + moved)
    return tallies[jax.random.permutation(jax.random.fold_in(rng, 2), amount)]


def normal_values(own_key, extent, width, most, cuts=(), kind=jnp.bfloat16):
    loudness = block_scale(own_key, extent, cuts, -0.22, 0.18) if cuts else 1.0
    values = jax.random.normal(own_key, extent, jnp.float32) * width * loudness
    return jnp.minimum(jnp.maximum(values, -most), most).astype(kind)


def setup_inputs(seed: int = 0) -> dict:
    arg_keys = jax.random.split(jax.random.key(seed), 11)
    query_nope = normal_values(arg_keys[0], (TOKENS, HEADS, NOPE), 1.0, 6.0, ((0, 256),))
    query_rope = draw_query_rope(jax.random.fold_in(arg_keys[10], 71), 0)
    out_grad = normal_values(arg_keys[2], (TOKENS, HEADS, NOPE), 1.0, 6.0, ((0, 256),))
    latent_rows = normal_values(arg_keys[3], (TOKENS, KV_WIDTH), 1.0, 6.0, ((0, 256),))
    prompt_latent = draw_prompt_latent(jax.random.fold_in(arg_keys[10], 71), 0)
    key_weight = normal_values(arg_keys[5], (HEADS, NOPE, LATENT), NOPE ** -0.5, 0.5, ((0, 16),))
    value_weight = normal_values(arg_keys[6], (HEADS, NOPE, LATENT), LATENT ** -0.5, 0.25, ((0, 16),))
    prompt_of = plant(jax.random.randint(arg_keys[7], (N_DP, N_SEQ), 0, PROMPTS), jax.random.fold_in(arg_keys[7], 1), 0, PROMPTS - 1).astype(jnp.int32)
    prompt_len = draw_prompt_len(jax.random.fold_in(arg_keys[10], 71), 0)
    response_ids = jax.vmap(lambda own: jnp.searchsorted(jnp.cumsum(uneven_parts(own, 4, TOK_DEV, TOK_DEV // 2, 2)), jnp.arange(TOK_DEV), side="right"))(jax.random.split(arg_keys[9], (N_DP * N_SEQ))).reshape((N_DP * N_SEQ, TOK_DEV)).astype(jnp.int32)
    return {"query_nope": query_nope, "query_rope": query_rope, "out_grad": out_grad, "latent_rows": latent_rows, "prompt_latent": prompt_latent, "key_weight": key_weight, "value_weight": value_weight, "prompt_of": prompt_of, "prompt_len": prompt_len, "response_ids": response_ids}


masked_score = -1e30


def widen(array):
    return array.astype(jnp.float32)


def device_grads(query_part, rope_part, grad_part, own_rows, seg_ids, prompt_rows, prompt_size, key_weight, value_weight):
    score_scale = (NOPE + ROPE) ** -0.5
    row_count = query_part.shape[0]
    all_keys = jnp.concatenate([prompt_rows, own_rows], 0)
    rope_three = rope_part.reshape(row_count, HEADS, ROPE)
    q_lat = jnp.einsum('thd,hdl->thl', widen(query_part), widen(key_weight)).astype(jnp.bfloat16)
    g_lat = jnp.einsum('thd,hdl->thl', widen(grad_part), widen(value_weight)).astype(jnp.bfloat16)
    positions = jnp.arange(row_count)
    prompt_ok = jnp.broadcast_to((jnp.arange(PROMPT) < prompt_size)[None, :], (row_count, PROMPT))
    own_ok = (positions[None, :] <= positions[:, None]) & (seg_ids[None, :] == seg_ids[:, None])
    key_mask = jnp.concatenate([prompt_ok, own_ok], 1)
    scores = jnp.einsum('thl,kl->htk', widen(q_lat), widen(all_keys[:, :LATENT]))
    scores = (scores + jnp.einsum('thr,kr->htk', widen(rope_three), widen(all_keys[:, LATENT:]))) * score_scale
    scores = jnp.where(key_mask[None], scores, masked_score)
    row_max = jnp.max(scores, -1, keepdims=True)
    shifted = jnp.exp(scores - row_max)
    prob_w = shifted / jnp.sum(shifted, -1, keepdims=True)
    dprob = jnp.einsum('thl,kl->htk', widen(g_lat), widen(all_keys[:, :LATENT]))
    delta = jnp.sum(prob_w * dprob, -1, keepdims=True)
    dscore = (prob_w * (dprob - delta) * score_scale).astype(jnp.bfloat16)
    prob_b = prob_w.astype(jnp.bfloat16)
    dquery = jnp.einsum('htk,kc->thc', widen(dscore), widen(all_keys))
    dq_lat = dquery[..., :LATENT].astype(jnp.bfloat16)
    grad_nope = jnp.einsum('thl,hdl->thd', widen(dq_lat), widen(key_weight)).astype(jnp.bfloat16)
    grad_rope = dquery[..., LATENT:].astype(jnp.bfloat16).reshape(row_count, HEADS * ROPE)
    full_query = jnp.concatenate([q_lat, rope_three], -1)
    dkey = jnp.einsum('htk,thc->kc', widen(dscore), widen(full_query))
    dvalue = jnp.einsum('htk,thl->kl', widen(prob_b), widen(g_lat))
    dkey = dkey + jnp.pad(dvalue, ((0, 0), (0, ROPE)))
    return grad_nope, grad_rope, dkey[PROMPT:].astype(jnp.bfloat16), dkey[:PROMPT]


def reference(query_nope, query_rope, out_grad, latent_rows, prompt_latent, key_weight, value_weight, prompt_of, prompt_len, response_ids):
    devices_all = N_DP * N_SEQ
    query_dev = query_nope.reshape(devices_all, TOK_DEV, HEADS, NOPE)
    rope_dev = query_rope.reshape(devices_all, TOK_DEV, HEADS * ROPE)
    grad_dev = out_grad.reshape(devices_all, TOK_DEV, HEADS, NOPE)
    rows_dev = latent_rows.reshape(devices_all, TOK_DEV, KV_WIDTH)
    table = prompt_of.reshape(devices_all).astype(jnp.int32)

    def device_step(totals, items):
        query_part, rope_part, grad_part, own_rows, seg_ids, which = items
        prompt_rows = lax.dynamic_index_in_dim(prompt_latent, which, 0, keepdims=False)
        prompt_size = lax.dynamic_index_in_dim(prompt_len, which, 0, keepdims=False)
        grad_nope, grad_rope, grad_own, grad_pre = device_grads(query_part, rope_part, grad_part, own_rows, seg_ids, prompt_rows, prompt_size, key_weight, value_weight)
        one_hot = (jnp.arange(PROMPTS) == which).astype(jnp.float32)
        totals = totals + one_hot[:, None, None] * grad_pre[None]
        return totals, (grad_nope, grad_rope, grad_own)

    start_totals = jnp.zeros((PROMPTS, PROMPT, KV_WIDTH), jnp.float32)
    totals, outputs = lax.scan(device_step, start_totals, (query_dev, rope_dev, grad_dev, rows_dev, response_ids, table))
    grad_nope, grad_rope, grad_own = outputs
    return (grad_nope.reshape(TOKENS, HEADS, NOPE), grad_rope.reshape(TOKENS, HEADS * ROPE), grad_own.reshape(TOKENS, KV_WIDTH), totals)
```

```python
import functools
import math

import jax
import jax.numpy as jnp
import numpy as np
from jax import lax
from jax.experimental import pallas as pl
from jax.experimental.pallas import tpu as pltpu
from jax.sharding import PartitionSpec as P

NOPE = 128
ROPE = 64
LATENT = 512
WIDTH = LATENT + ROPE
SCALE = (NOPE + ROPE) ** -0.5
LOG2E = math.log2(math.e)
MASKED = -1e30
AXES = ("dp", "seq")
NX, NY, NZ_HI, NZ_LO, NCORE = 4, 4, 2, 4, 2
NZ = NZ_HI * NZ_LO
PPS = 4
F32 = jnp.float32
BF16 = jnp.bfloat16


def place(i):
    x, z_lo = i % NX, i // NX % NZ_LO
    core, z_hi, y = i // 16 % NCORE, i // 32 % NZ_HI, i // 64
    return x, y, z_hi * NZ_LO + z_lo, core


def number(x, y, z, core):
    x, y, z, core = x % NX, y % NY, z % NZ, core % NCORE
    return ((y * NZ_HI + z // NZ_LO) * NCORE + core) * 16 + z % NZ_LO * NX + x


def permute(array, move):
    pairs = []
    for i in range(NX * NY * NZ * NCORE):
        x, y, z, core = place(i)
        dx, dz, dc = move(core)
        pairs.append((i, number(x + dx, y, z + dz, core + dc)))
    return lax.ppermute(array, AXES, pairs)


def swap(array):
    return permute(array, lambda core: (0, 0, 1))


def first_ring(array, step):
    return permute(array, lambda core: (0, step, 0) if core else (step, 0, 0))


def second_ring(array, step):
    return permute(array, lambda core: (step, 0, 0) if core else (0, step, 0))


def nt(a, b):
    return lax.dot_general(a, b, (((1,), (1,)), ((), ())), preferred_element_type=F32)


def tn(a, b):
    return lax.dot_general(a, b, (((0,), (0,)), ((), ())), preferred_element_type=F32)


def nn(a, b):
    return jnp.dot(a, b, preferred_element_type=F32)


def attention_kernel(counts, first, last, pair_ref, prompt_of_ref, prompt_len_ref, *refs):
    sources = len(counts)
    source_refs, refs = refs[:sources], refs[sources:]
    q_refs, refs = refs[:PPS], refs[PPS:]
    g_refs, refs = refs[:PPS], refs[PPS:]
    rope_refs, refs = refs[:PPS], refs[PPS:]
    (prompt_ref, own_ref, own_bias_ref), refs = refs[:3], refs[3:]
    if not first:
        (lat_in, turn_in), refs = refs[:2], refs[4:]
    (first_out, second_out, nope_out, rope_out), refs = refs[:4], refs[4:]
    if last:
        (lat_ref, turn_ref), refs = refs[:2], refs[2:]
    else:
        lat_ref, turn_ref = first_out, second_out
    latent_ref, rot_ref, bias_ref, weights, nope_part, rope_part, sems, weight_sems = refs
    step = pl.program_id(0)
    steps = pl.num_programs(0)
    slot = lax.rem(step, 2)

    tokens, prompts = own_ref.shape[0], prompt_ref.shape[0]

    @pl.when(step == 0)
    def _():
        for begin, rows_ref in ((0, prompt_ref), (prompts, own_ref)):
            here = pl.ds(begin, rows_ref.shape[0])
            latent_ref[here, :] = rows_ref[:, :LATENT]
            rotary = rows_ref[:, LATENT:]
            rot_ref[here, :] = jnp.concatenate([rotary, rotary], 1)
        live = prompt_len_ref[prompt_of_ref[lax.axis_index("dp"), lax.axis_index("seq")]]
        row = lax.broadcasted_iota(jnp.int32, (prompts, 2 * tokens), 0)
        bias_ref[:prompts, :] = jnp.where(row < live, 0.0, MASKED).astype(F32)
        own_bias = own_bias_ref[...]
        bias_ref[prompts:, :] = jnp.concatenate([own_bias, own_bias], 1)
        if first:
            lat_ref[...] = jnp.zeros_like(lat_ref)
            turn_ref[...] = jnp.zeros_like(turn_ref)
        else:
            lat_ref[...] = lat_in[...]
            turn_ref[...] = turn_in[...]

    def fetch(at):
        begin = 0
        for k in range(sources):
            ahead, lane_of = begin // PPS, begin % PPS

            @pl.when(at == ahead)
            def _(k=k, lane_of=lane_of):
                here = weights.at[at % 2, pl.ds(lane_of, counts[k])]
                pltpu.make_async_copy(source_refs[k], here, weight_sems.at[at % 2]).start()

            begin += counts[k]

    @pl.when(step == 0)
    def _():
        fetch(step)

    @pl.when(step + 1 < steps)
    def _():
        fetch(step + 1)

    pltpu.make_async_copy(weights.at[slot], weights.at[slot], weight_sems.at[slot]).wait()

    def copies(at, where):
        out = []
        for p in range(PPS):
            pair = pair_ref[at * PPS + p]
            out.append(pltpu.make_async_copy(nope_part.at[where, p], nope_out.at[pair], sems.at[where, 0, p]))
            lanes = pl.ds(pl.multiple_of(pair * 2 * ROPE, 2 * ROPE), 2 * ROPE)
            out.append(pltpu.make_async_copy(rope_part.at[where, p], rope_out.at[:, lanes], sems.at[where, 1, p]))
        return out

    @pl.when(step >= 2)
    def _():
        for copy in copies(step - 2, slot):
            copy.wait()

    latent = latent_ref[...]
    rot = rot_ref[...]
    bias = bias_ref[...]
    lane = lax.broadcasted_iota(jnp.int32, (tokens, 2 * ROPE), 1) // ROPE
    mine = lane == 0
    none = jnp.zeros((tokens, NOPE), BF16)
    zero = jnp.zeros((tokens, 2 * ROPE), BF16)
    kept = [{} for _ in range(PPS)]

    def project(p):
        up = nt(latent, weights[slot, p].reshape(4 * NOPE, LATENT)).astype(BF16)
        kept[p]["keys"] = jnp.concatenate([up[:, :256], rot], 1)
        kept[p]["values"] = up[:, 256:]

    def compare(p):
        q0, q1 = q_refs[p][0, 0], q_refs[p][0, 1]
        g0, g1 = g_refs[p][0, 0], g_refs[p][0, 1]
        rope = rope_refs[p][...]
        rope0, rope1 = jnp.where(mine, rope, zero), jnp.where(mine, zero, rope)
        kept[p]["queries"] = jnp.concatenate(
            [jnp.concatenate([q0, none, rope0], 1), jnp.concatenate([none, q1, rope1], 1)], 0
        )
        kept[p]["out_grad"] = jnp.concatenate(
            [jnp.concatenate([g0, none], 1), jnp.concatenate([none, g1], 1)], 0
        )
        keys = kept[p]["keys"]
        score0 = nt(jnp.concatenate([keys[:, :128], rot], 1), jnp.concatenate([q0, rope0], 1))
        score1 = nt(keys[:, 128:], jnp.concatenate([q1, rope1], 1))
        kept[p]["score"] = jnp.concatenate([score0, score1], 1)
        kept[p]["dprob"] = nt(kept[p]["values"], kept[p]["out_grad"])

    def soften(p):
        score = kept[p]["score"] * (SCALE * LOG2E) + bias
        dprob = kept[p]["dprob"]
        top = jnp.max(score, 0, keepdims=True)
        e = jnp.exp2(score - top)
        inverse = 1.0 / jnp.sum(e, 0, keepdims=True)
        delta = jnp.sum(e * dprob, 0, keepdims=True) * inverse
        prob = e * inverse
        kept[p]["prob"] = prob.astype(BF16)
        kept[p]["dscore"] = (prob * (dprob - delta) * SCALE).astype(BF16)

    def derive(p):
        keys, dscore = kept[p]["keys"], kept[p]["dscore"]
        dkeys = nn(dscore, kept[p]["queries"])
        dvalues = nn(kept[p]["prob"], kept[p]["out_grad"])
        kept[p]["turn"] = dkeys[:, 256:]
        kept[p]["grads"] = [dkeys[:, :256].astype(BF16), dvalues.astype(BF16)]
        dq0 = tn(dscore[:, :tokens], jnp.concatenate([keys[:, :128], rot], 1))
        dq1 = tn(dscore[:, tokens:], jnp.concatenate([keys[:, 128:256], rot], 1))
        nope_part[slot, p, 0] = dq0[:, :128].astype(BF16)
        nope_part[slot, p, 1] = dq1[:, :128].astype(BF16)
        rope_part[slot, p] = jnp.where(mine, dq0[:, 128:], dq1[:, 128:]).astype(BF16)

    stages = (project, compare, soften, derive)
    for tick in range(PPS + len(stages) - 1):
        for k in range(len(stages)):
            if 0 <= tick - k < PPS:
                stages[k](tick - k)
    turn_ref[...] += sum(kept[p]["turn"] for p in range(PPS))
    lat_ref[...] += nn(jnp.concatenate(sum([kept[p]["grads"] for p in range(PPS)], []), 1), weights[slot].reshape(PPS * 4 * NOPE, LATENT))

    for copy in copies(step, slot):
        copy.start()

    if last:

        @pl.when(step == steps - 1)
        def _():
            prompts = first_out.shape[0]
            turned = turn_ref[:, :ROPE] + turn_ref[:, ROPE:]
            total = jnp.concatenate([lat_ref[...], turned], 1)
            first_out[...] = total[:prompts]
            second_out[...] = total[prompts:].astype(BF16)

    @pl.when(step == steps - 1)
    def _():
        if total_steps(counts) > 1:
            for copy in copies(step - 1, 1 - slot):
                copy.wait()
        for copy in copies(step, slot):
            copy.wait()


def total_steps(counts):
    return sum(counts) // PPS


def attention(sources, scalars, q, g, rope, prompt, own, own_bias, state, last=False):
    counts = tuple(source.shape[0] for source in sources)
    first = state is None
    steps = total_steps(counts)
    tokens = own.shape[0]
    keys = prompt.shape[0] + tokens
    any_spec = pl.BlockSpec(memory_space=pl.ANY)

    head_specs = [
        pl.BlockSpec((1, 2, tokens, NOPE), lambda i, pair, *_, p=p: (pair[i * PPS + p], 0, 0, 0))
        for p in range(PPS)
    ]
    rope_specs = [
        pl.BlockSpec((tokens, 2 * ROPE), lambda i, pair, *_, p=p: (0, pair[i * PPS + p])) for p in range(PPS)
    ]

    def whole(shape):
        return pl.BlockSpec(shape, lambda i, *_: (0,) * len(shape))

    in_specs = [any_spec] * len(sources) + head_specs * 2 + rope_specs
    in_specs += [whole(prompt.shape), whole(own.shape), whole(own_bias.shape)]
    operands = list(sources)
    operands += [q] * PPS + [g] * PPS + [rope] * PPS + [prompt, own, own_bias]
    aliases = {}
    if not first:
        operands += list(state)
        in_specs += [whole((keys, LATENT)), whole((keys, 2 * ROPE)), any_spec, any_spec]
        aliases = {len(scalars) + len(operands) - 2: 2, len(scalars) + len(operands) - 1: 3}
    sums = (jax.ShapeDtypeStruct((keys, LATENT), F32), jax.ShapeDtypeStruct((keys, 2 * ROPE), F32))
    sum_scratch = []
    if last:
        sum_scratch = [pltpu.VMEM(s.shape, F32) for s in sums]
        sums = (jax.ShapeDtypeStruct((keys - tokens, WIDTH), F32), jax.ShapeDtypeStruct((tokens, WIDTH), BF16))
    return pl.pallas_call(
        functools.partial(attention_kernel, counts, first, last),
        out_shape=(
            *sums,
            jax.ShapeDtypeStruct(q.shape, BF16),
            jax.ShapeDtypeStruct(rope.shape, BF16),
        ),
        grid_spec=pltpu.PrefetchScalarGridSpec(
            num_scalar_prefetch=len(scalars),
            grid=(steps,),
            in_specs=in_specs,
            out_specs=(whole(sums[0].shape), whole(sums[1].shape), any_spec, any_spec),
            scratch_shapes=sum_scratch
            + [
                pltpu.VMEM((keys, LATENT), BF16),
                pltpu.VMEM((keys, 2 * ROPE), BF16),
                pltpu.VMEM((keys, 2 * tokens), F32),
                pltpu.VMEM((2, PPS, 2, 2, NOPE, LATENT), BF16),
                pltpu.VMEM((2, PPS, 2, tokens, NOPE), BF16),
                pltpu.VMEM((2, PPS, tokens, 2 * ROPE), BF16),
                pltpu.SemaphoreType.DMA((2, 2, PPS)),
                pltpu.SemaphoreType.DMA((2,)),
            ],
        ),
        input_output_aliases=aliases,
        compiler_params=pltpu.CompilerParams(vmem_limit_bytes=48 * 1024 * 1024),
        name="attention",
    )(*scalars, *operands)


def halves_kernel(low_in, high_in, _, low, high):
    low[...] = low_in[...]
    high[...] = high_in[...]


def halves(low, high, before):
    n, *rest = low.shape
    n //= 2

    def block(begin):
        return pl.BlockSpec((1, *rest), lambda i: (begin + i,) + (0,) * len(rest))

    shape = jax.ShapeDtypeStruct((n, *rest), low.dtype)
    return pl.pallas_call(
        halves_kernel,
        out_shape=(shape, shape),
        grid=(n,),
        in_specs=[block(0), block(n), pl.BlockSpec(memory_space=pl.ANY)],
        out_specs=[block(0), block(0)],
        name="halves",
    )(low, high, before)


def small_call(kernel, prompt_of, rows, dtype, scratch, name):
    block = pl.BlockSpec(rows.shape, lambda i, *_: (0, 0, 0))
    return pl.pallas_call(
        kernel,
        out_shape=jax.ShapeDtypeStruct(rows.shape, dtype),
        grid_spec=pltpu.PrefetchScalarGridSpec(
            num_scalar_prefetch=1, grid=(1,), in_specs=[block], out_specs=block, scratch_shapes=scratch
        ),
        name=name,
    )(prompt_of, rows)


def select_kernel(prompt_ref, rows_ref, out_ref):
    group = lax.axis_index("dp")
    for m in range(rows_ref.shape[0]):
        out_ref[m] = rows_ref[prompt_ref[group, m]]


def select(prompt_of, rows):
    return small_call(select_kernel, prompt_of, rows, rows.dtype, [], "select")


def collect_kernel(prompt_ref, parts_ref, out_ref, sums):
    group = lax.axis_index("dp")
    sums[...] = jnp.zeros_like(sums)
    for m in range(parts_ref.shape[0]):
        sums[prompt_ref[group, m]] += parts_ref[m]
    out_ref[...] = sums[...].astype(out_ref.dtype)


def collect(prompt_of, parts):
    return small_call(collect_kernel, prompt_of, parts, BF16, [pltpu.VMEM(parts.shape, F32)], "collect")


def local(
    query_nope,
    query_rope,
    out_grad,
    latent_rows,
    prompt_latent,
    key_weight,
    value_weight,
    prompt_of,
    prompt_len,
    response_ids,
):
    dp, seq = lax.axis_index("dp"), lax.axis_index("seq")
    members = lax.axis_size("seq")
    core = dp % NCORE
    z_lo, x = seq // NX, seq % NX
    tokens, heads = query_nope.shape[:2]
    rows = prompt_latent.shape[1]
    prompts = members * rows

    with jax.named_scope("weights_first_ring"):
        both = jnp.stack([key_weight.reshape(2, 2, NOPE, LATENT), value_weight.reshape(2, 2, NOPE, LATENT)], 1)
        here = lax.dynamic_index_in_dim(both, core, 0, keepdims=False)
        before, after = first_ring(here, 1), first_ring(here, -1)
        opposite = jnp.stack([first_ring(here[0], 2), first_ring(here[1], -2)])

    with jax.named_scope("prompt_gather"):
        copies = jnp.broadcast_to(prompt_latent, (members, rows, WIDTH))
        column = lax.all_to_all(copies, "dp", 0, 0, tiled=True)

    with jax.named_scope("weights_second_ring"):
        near = jnp.stack([here, before, after, opposite])
        near, column = lax.optimization_barrier((near, column))
        middle = [second_ring(near, 1), second_ring(near, -1)]
        near_peer = swap(near)

    with jax.named_scope("prompt_exchange"):
        prompt_rows = lax.all_to_all(select(prompt_of, column), "seq", 0, 0, tiled=True).reshape(prompts, WIDTH)

    with jax.named_scope("pair_numbers"):
        order = (0, -1, 1, 2)

        def numbers(side, *blocks):
            table = np.array([(a, far) for far, nears in blocks for a in nears], np.int32)
            kind = core ^ side
            dx = jnp.where(kind == 0, table[:, 0], table[:, 1])
            dz = jnp.where(kind == 0, table[:, 1], table[:, 0])
            return (((z_lo + dz) & 3) * NX + ((x + dx) & 3)) * 2 + kind

        first_pairs = jnp.concatenate([numbers(0, (0, order)), numbers(1, (0, order)), numbers(0, (-1, order), (1, order))])
        peer_pairs = numbers(1, (-1, order), (1, order))
        far_pairs = jnp.concatenate([numbers(side, (2, order[:2]), (2, order[2:])) for side in range(2)])

    q = query_nope.reshape(tokens, heads // 2, 2, NOPE).transpose(1, 2, 0, 3)
    g = out_grad.reshape(tokens, heads // 2, 2, NOPE).transpose(1, 2, 0, 3)
    ids = response_ids[0]
    t = jnp.arange(tokens)
    own_ok = (t[:, None] <= t[None, :]) & (ids[:, None] == ids[None, :])
    own_bias = jnp.where(own_ok, 0.0, MASKED).astype(F32)

    def work(sources, pairs, state, last=False):
        scalars = (pairs, prompt_of, prompt_len)
        return attention(sources, scalars, q, g, query_rope, prompt_rows, latent_rows, own_bias, state, last)

    with jax.named_scope("weights_opposite"):
        *middle, low, high = lax.optimization_barrier((*middle, *halves(*middle, prompt_rows)))
        far = [second_ring(low, 1), second_ring(high, -1)]
        middle_peer = [swap(w) for w in middle]
    state = work([near, near_peer, *middle], first_pairs, None)
    *far, turn = lax.optimization_barrier((*far, state[1]))
    state = (state[0], turn, *state[2:])
    far_peer = [swap(w) for w in far]
    state = work(middle_peer, peer_pairs, state)
    prompt_part, grad_latent, grad_nope, grad_rope = work([*far, *far_peer], far_pairs, state, last=True)

    with jax.named_scope("prompt_return"):
        parts = lax.all_to_all(prompt_part.reshape(members, rows, WIDTH), "seq", 0, 0, tiled=True)
        sums = lax.all_to_all(collect(prompt_of, parts), "dp", 0, 0, tiled=True)
        owned = jnp.sum(sums.astype(F32), 0, keepdims=True)

    grad_nope = grad_nope.transpose(2, 0, 1, 3).reshape(tokens, heads, NOPE)
    return grad_nope, grad_rope, grad_latent, owned


def solution(mesh):
    return jax.shard_map(
        local,
        mesh=mesh,
        in_specs=(
            P(AXES, None, None),
            P(AXES, None),
            P(AXES, None, None),
            P(AXES, None),
            P("dp", "seq", None),
            P("seq", None, None),
            P("seq", None, None),
            P(),
            P(),
            P(AXES, None),
        ),
        out_specs=(
            P(AXES, None, None),
            P(AXES, None),
            P(AXES, None),
            P("dp", "seq", None),
        ),
        check_vma=False,
    )
```

```python
import functools
import math

import jax
import jax.numpy as jnp
import numpy as np
from jax import lax
from jax.experimental import pallas as pl
from jax.experimental.pallas import tpu as pltpu
from jax.sharding import PartitionSpec as P

NOPE = 128
ROPE = 64
LATENT = 512
WIDTH = LATENT + ROPE
SCALE = (NOPE + ROPE) ** -0.5
LOG2E = math.log2(math.e)
MASKED = -1e30
AXES = ("dp", "seq")
NX, NY, NZ_HI, NZ_LO, NCORE = 4, 4, 2, 4, 2
NZ = NZ_HI * NZ_LO
PPS = 4
F32 = jnp.float32
BF16 = jnp.bfloat16


def place(i):
    x, z_lo = i % NX, i // NX % NZ_LO
    core, z_hi, y = i // 16 % NCORE, i // 32 % NZ_HI, i // 64
    return x, y, z_hi * NZ_LO + z_lo, core


def number(x, y, z, core):
    x, y, z, core = x % NX, y % NY, z % NZ, core % NCORE
    return ((y * NZ_HI + z // NZ_LO) * NCORE + core) * 16 + z % NZ_LO * NX + x


def permute(array, move):
    pairs = []
    for i in range(NX * NY * NZ * NCORE):
        x, y, z, core = place(i)
        dx, dz, dc = move(core)
        pairs.append((i, number(x + dx, y, z + dz, core + dc)))
    return lax.ppermute(array, AXES, pairs)


def swap(array):
    return permute(array, lambda core: (0, 0, 1))


def first_ring(array, step):
    return permute(array, lambda core: (0, step, 0) if core else (step, 0, 0))


def second_ring(array, step):
    return permute(array, lambda core: (step, 0, 0) if core else (0, step, 0))


def nt(a, b):
    return lax.dot_general(a, b, (((1,), (1,)), ((), ())), preferred_element_type=F32)


def tn(a, b):
    return lax.dot_general(a, b, (((0,), (0,)), ((), ())), preferred_element_type=F32)


def nn(a, b):
    return jnp.dot(a, b, preferred_element_type=F32)


def attention_kernel(counts, first, last, pair_ref, prompt_of_ref, prompt_len_ref, *refs):
    sources = len(counts)
    source_refs, refs = refs[:sources], refs[sources:]
    q_refs, refs = refs[:PPS], refs[PPS:]
    g_refs, refs = refs[:PPS], refs[PPS:]
    rope_refs, refs = refs[:PPS], refs[PPS:]
    (prompt_ref, own_ref, own_bias_ref), refs = refs[:3], refs[3:]
    if not first:
        (lat_in, turn_in), refs = refs[:2], refs[4:]
    (first_out, second_out, nope_out, rope_out), refs = refs[:4], refs[4:]
    if last:
        (lat_ref, turn_ref), refs = refs[:2], refs[2:]
    else:
        lat_ref, turn_ref = first_out, second_out
    latent_ref, rot_ref, bias_ref, weights, nope_part, rope_part, sems, weight_sems = refs
    step = pl.program_id(0)
    steps = pl.num_programs(0)
    slot = lax.rem(step, 2)

    tokens, prompts = own_ref.shape[0], prompt_ref.shape[0]

    @pl.when(step == 0)
    def _():
        for begin, rows_ref in ((0, prompt_ref), (prompts, own_ref)):
            here = pl.ds(begin, rows_ref.shape[0])
            latent_ref[here, :] = rows_ref[:, :LATENT]
            rotary = rows_ref[:, LATENT:]
            rot_ref[here, :] = jnp.concatenate([rotary, rotary], 1)
        live = prompt_len_ref[prompt_of_ref[lax.axis_index("dp"), lax.axis_index("seq")]]
        row = lax.broadcasted_iota(jnp.int32, (prompts, 2 * tokens), 0)
        bias_ref[:prompts, :] = jnp.where(row < live, 0.0, MASKED).astype(F32)
        own_bias = own_bias_ref[...]
        bias_ref[prompts:, :] = jnp.concatenate([own_bias, own_bias], 1)
        if first:
            lat_ref[...] = jnp.zeros_like(lat_ref)
            turn_ref[...] = jnp.zeros_like(turn_ref)
        else:
            lat_ref[...] = lat_in[...]
            turn_ref[...] = turn_in[...]

    def fetch(at):
        begin = 0
        for k in range(sources):
            ahead, lane_of = begin // PPS, begin % PPS

            @pl.when(at == ahead)
            def _(k=k, lane_of=lane_of):
                here = weights.at[at % 2, pl.ds(lane_of, counts[k])]
                pltpu.make_async_copy(source_refs[k], here, weight_sems.at[at % 2]).start()

            begin += counts[k]

    @pl.when(step == 0)
    def _():
        fetch(step)

    @pl.when(step + 1 < steps)
    def _():
        fetch(step + 1)

    pltpu.make_async_copy(weights.at[slot], weights.at[slot], weight_sems.at[slot]).wait()

    def copies(at, where):
        out = []
        for p in range(PPS):
            pair = pair_ref[at * PPS + p]
            out.append(pltpu.make_async_copy(nope_part.at[where, p], nope_out.at[pair], sems.at[where, 0, p]))
            lanes = pl.ds(pl.multiple_of(pair * 2 * ROPE, 2 * ROPE), 2 * ROPE)
            out.append(pltpu.make_async_copy(rope_part.at[where, p], rope_out.at[:, lanes], sems.at[where, 1, p]))
        return out

    @pl.when(step >= 2)
    def _():
        for copy in copies(step - 2, slot):
            copy.wait()

    latent = latent_ref[...]
    rot = rot_ref[...]
    bias = bias_ref[...]
    lane = lax.broadcasted_iota(jnp.int32, (tokens, 2 * ROPE), 1) // ROPE
    mine = lane == 0
    none = jnp.zeros((tokens, NOPE), BF16)
    zero = jnp.zeros((tokens, 2 * ROPE), BF16)
    kept = [{} for _ in range(PPS)]

    def project(p):
        up = nt(latent, weights[slot, p].reshape(4 * NOPE, LATENT)).astype(BF16)
        kept[p]["keys"] = jnp.concatenate([up[:, :256], rot], 1)
        kept[p]["values"] = up[:, 256:]

    def compare(p):
        q0, q1 = q_refs[p][0, 0], q_refs[p][0, 1]
        g0, g1 = g_refs[p][0, 0], g_refs[p][0, 1]
        rope = rope_refs[p][...]
        rope0, rope1 = jnp.where(mine, rope, zero), jnp.where(mine, zero, rope)
        kept[p]["queries"] = jnp.concatenate(
            [jnp.concatenate([q0, none, rope0], 1), jnp.concatenate([none, q1, rope1], 1)], 0
        )
        kept[p]["out_grad"] = jnp.concatenate(
            [jnp.concatenate([g0, none], 1), jnp.concatenate([none, g1], 1)], 0
        )
        keys = kept[p]["keys"]
        score0 = nt(jnp.concatenate([keys[:, :128], rot], 1), jnp.concatenate([q0, rope0], 1))
        score1 = nt(keys[:, 128:], jnp.concatenate([q1, rope1], 1))
        kept[p]["score"] = jnp.concatenate([score0, score1], 1)
        kept[p]["dprob"] = nt(kept[p]["values"], kept[p]["out_grad"])

    def soften(p):
        score = kept[p]["score"] * (SCALE * LOG2E) + bias
        dprob = kept[p]["dprob"]
        top = jnp.max(score, 0, keepdims=True)
        e = jnp.exp2(score - top)
        inverse = 1.0 / jnp.sum(e, 0, keepdims=True)
        delta = jnp.sum(e * dprob, 0, keepdims=True) * inverse
        prob = e * inverse
        kept[p]["prob"] = prob.astype(BF16)
        kept[p]["dscore"] = (prob * (dprob - delta) * SCALE).astype(BF16)

    def derive(p):
        keys, dscore = kept[p]["keys"], kept[p]["dscore"]
        dkeys = nn(dscore, kept[p]["queries"])
        dvalues = nn(kept[p]["prob"], kept[p]["out_grad"])
        kept[p]["turn"] = dkeys[:, 256:]
        kept[p]["grads"] = [dkeys[:, :256].astype(BF16), dvalues.astype(BF16)]
        dq0 = tn(dscore[:, :tokens], jnp.concatenate([keys[:, :128], rot], 1))
        dq1 = tn(dscore[:, tokens:], jnp.concatenate([keys[:, 128:256], rot], 1))
        nope_part[slot, p, 0] = dq0[:, :128].astype(BF16)
        nope_part[slot, p, 1] = dq1[:, :128].astype(BF16)
        rope_part[slot, p] = jnp.where(mine, dq0[:, 128:], dq1[:, 128:]).astype(BF16)

    stages = (project, compare, soften, derive)
    for tick in range(PPS + len(stages) - 1):
        for k in range(len(stages)):
            if 0 <= tick - k < PPS:
                stages[k](tick - k)
    turn_ref[...] += sum(kept[p]["turn"] for p in range(PPS))
    lat_ref[...] += nn(jnp.concatenate(sum([kept[p]["grads"] for p in range(PPS)], []), 1), weights[slot].reshape(PPS * 4 * NOPE, LATENT))

    for copy in copies(step, slot):
        copy.start()

    if last:

        @pl.when(step == steps - 1)
        def _():
            prompts = first_out.shape[0]
            turned = turn_ref[:, :ROPE] + turn_ref[:, ROPE:]
            total = jnp.concatenate([lat_ref[...], turned], 1)
            first_out[...] = total[:prompts]
            second_out[...] = total[prompts:].astype(BF16)

    @pl.when(step == steps - 1)
    def _():
        if total_steps(counts) > 1:
            for copy in copies(step - 1, 1 - slot):
                copy.wait()
        for copy in copies(step, slot):
            copy.wait()


def total_steps(counts):
    return sum(counts) // PPS


def attention(sources, scalars, q, g, rope, prompt, own, own_bias, state, last=False):
    counts = tuple(source.shape[0] for source in sources)
    first = state is None
    steps = total_steps(counts)
    tokens = own.shape[0]
    keys = prompt.shape[0] + tokens
    any_spec = pl.BlockSpec(memory_space=pl.ANY)

    head_specs = [
        pl.BlockSpec((1, 2, tokens, NOPE), lambda i, pair, *_, p=p: (pair[i * PPS + p], 0, 0, 0))
        for p in range(PPS)
    ]
    rope_specs = [
        pl.BlockSpec((tokens, 2 * ROPE), lambda i, pair, *_, p=p: (0, pair[i * PPS + p])) for p in range(PPS)
    ]

    def whole(shape):
        return pl.BlockSpec(shape, lambda i, *_: (0,) * len(shape))

    in_specs = [any_spec] * len(sources) + head_specs * 2 + rope_specs
    in_specs += [whole(prompt.shape), whole(own.shape), whole(own_bias.shape)]
    operands = list(sources)
    operands += [q] * PPS + [g] * PPS + [rope] * PPS + [prompt, own, own_bias]
    aliases = {}
    if not first:
        operands += list(state)
        in_specs += [whole((keys, LATENT)), whole((keys, 2 * ROPE)), any_spec, any_spec]
        aliases = {len(scalars) + len(operands) - 2: 2, len(scalars) + len(operands) - 1: 3}
    sums = (jax.ShapeDtypeStruct((keys, LATENT), F32), jax.ShapeDtypeStruct((keys, 2 * ROPE), F32))
    sum_scratch = []
    if last:
        sum_scratch = [pltpu.VMEM(s.shape, F32) for s in sums]
        sums = (jax.ShapeDtypeStruct((keys - tokens, WIDTH), F32), jax.ShapeDtypeStruct((tokens, WIDTH), BF16))
    return pl.pallas_call(
        functools.partial(attention_kernel, counts, first, last),
        out_shape=(
            *sums,
            jax.ShapeDtypeStruct(q.shape, BF16),
            jax.ShapeDtypeStruct(rope.shape, BF16),
        ),
        grid_spec=pltpu.PrefetchScalarGridSpec(
            num_scalar_prefetch=len(scalars),
            grid=(steps,),
            in_specs=in_specs,
            out_specs=(whole(sums[0].shape), whole(sums[1].shape), any_spec, any_spec),
            scratch_shapes=sum_scratch
            + [
                pltpu.VMEM((keys, LATENT), BF16),
                pltpu.VMEM((keys, 2 * ROPE), BF16),
                pltpu.VMEM((keys, 2 * tokens), F32),
                pltpu.VMEM((2, PPS, 2, 2, NOPE, LATENT), BF16),
                pltpu.VMEM((2, PPS, 2, tokens, NOPE), BF16),
                pltpu.VMEM((2, PPS, tokens, 2 * ROPE), BF16),
                pltpu.SemaphoreType.DMA((2, 2, PPS)),
                pltpu.SemaphoreType.DMA((2,)),
            ],
        ),
        input_output_aliases=aliases,
        compiler_params=pltpu.CompilerParams(vmem_limit_bytes=48 * 1024 * 1024),
        name="attention",
    )(*scalars, *operands)


def small_call(kernel, prompt_of, rows, dtype, scratch, name):
    block = pl.BlockSpec(rows.shape, lambda i, *_: (0, 0, 0))
    return pl.pallas_call(
        kernel,
        out_shape=jax.ShapeDtypeStruct(rows.shape, dtype),
        grid_spec=pltpu.PrefetchScalarGridSpec(
            num_scalar_prefetch=1, grid=(1,), in_specs=[block], out_specs=block, scratch_shapes=scratch
        ),
        name=name,
    )(prompt_of, rows)


def select_kernel(prompt_ref, rows_ref, out_ref):
    group = lax.axis_index("dp")
    for m in range(rows_ref.shape[0]):
        out_ref[m] = rows_ref[prompt_ref[group, m]]


def select(prompt_of, rows):
    return small_call(select_kernel, prompt_of, rows, rows.dtype, [], "select")


def collect_kernel(prompt_ref, parts_ref, out_ref, sums):
    group = lax.axis_index("dp")
    sums[...] = jnp.zeros_like(sums)
    for m in range(parts_ref.shape[0]):
        sums[prompt_ref[group, m]] += parts_ref[m]
    out_ref[...] = sums[...].astype(out_ref.dtype)


def collect(prompt_of, parts):
    return small_call(collect_kernel, prompt_of, parts, BF16, [pltpu.VMEM(parts.shape, F32)], "collect")


def local(
    query_nope,
    query_rope,
    out_grad,
    latent_rows,
    prompt_latent,
    key_weight,
    value_weight,
    prompt_of,
    prompt_len,
    response_ids,
):
    dp, seq = lax.axis_index("dp"), lax.axis_index("seq")
    members = lax.axis_size("seq")
    core = dp % NCORE
    z_lo, x = seq // NX, seq % NX
    tokens, heads = query_nope.shape[:2]
    rows = prompt_latent.shape[1]
    prompts = members * rows

    with jax.named_scope("weights_first_ring"):
        both = jnp.stack([key_weight.reshape(2, 2, NOPE, LATENT), value_weight.reshape(2, 2, NOPE, LATENT)], 1)
        here = lax.dynamic_index_in_dim(both, core, 0, keepdims=False)
        before, after = first_ring(here, 1), first_ring(here, -1)
        opposite = jnp.stack([first_ring(here[0], 2), first_ring(here[1], -2)])

    with jax.named_scope("prompt_gather"):
        copies = jnp.broadcast_to(prompt_latent, (members, rows, WIDTH))
        column = lax.all_to_all(copies, "dp", 0, 0, tiled=True)

    with jax.named_scope("weights_second_ring"):
        low, high = jnp.stack([here, before]), jnp.stack([after, opposite])
        low, high, column = lax.optimization_barrier((low, high, column))
        lead = [second_ring(low, 1), second_ring(high, -1)]
        near_peer = [swap(low), swap(high)]

    with jax.named_scope("prompt_exchange"):
        prompt_rows = lax.all_to_all(select(prompt_of, column), "seq", 0, 0, tiled=True).reshape(prompts, WIDTH)

    with jax.named_scope("pair_numbers"):
        order = (0, -1, 1, 2)

        def numbers(side, *blocks):
            table = np.array([(a, far) for far, nears in blocks for a in nears], np.int32)
            kind = core ^ side
            dx = jnp.where(kind == 0, table[:, 0], table[:, 1])
            dz = jnp.where(kind == 0, table[:, 1], table[:, 0])
            return (((z_lo + dz) & 3) * NX + ((x + dx) & 3)) * 2 + kind

        near_pairs = jnp.concatenate([numbers(side, (0, order)) for side in range(2)])
        lead_pairs = jnp.concatenate([numbers(side, (-1, order[:2]), (1, order[2:])) for side in range(2)])
        rest_blocks = (-1, order[2:]), (1, order[:2]), (2, order[:2]), (2, order[2:])
        rest_pairs = [numbers(side, *rest_blocks) for side in range(2)]

    q = query_nope.reshape(tokens, heads // 2, 2, NOPE).transpose(1, 2, 0, 3)
    g = out_grad.reshape(tokens, heads // 2, 2, NOPE).transpose(1, 2, 0, 3)
    ids = response_ids[0]
    t = jnp.arange(tokens)
    own_ok = (t[:, None] <= t[None, :]) & (ids[:, None] == ids[None, :])
    own_bias = jnp.where(own_ok, 0.0, MASKED).astype(F32)

    def work(sources, pairs, state, last=False):
        scalars = (pairs, prompt_of, prompt_len)
        return attention(sources, scalars, q, g, query_rope, prompt_rows, latent_rows, own_bias, state, last)

    with jax.named_scope("weights_rest"):
        low, high, *lead, prompt_rows = lax.optimization_barrier((low, high, *lead, prompt_rows))
        rest = [second_ring(high, 1), second_ring(low, -1), second_ring(lead[0], 1), second_ring(lead[1], -1)]
        lead_peer = [swap(w) for w in lead]
    state = work([low, high, *near_peer], near_pairs, None)
    state = work([*lead, *lead_peer], lead_pairs, state)
    *rest, turn = lax.optimization_barrier((*rest, state[1]))
    state = (state[0], turn, *state[2:])
    rest_peer = [swap(w) for w in rest]
    state = work(rest, rest_pairs[0], state)
    prompt_part, grad_latent, grad_nope, grad_rope = work(rest_peer, rest_pairs[1], state, last=True)

    with jax.named_scope("prompt_return"):
        parts = lax.all_to_all(prompt_part.reshape(members, rows, WIDTH), "seq", 0, 0, tiled=True)
        sums = lax.all_to_all(collect(prompt_of, parts), "dp", 0, 0, tiled=True)
        owned = jnp.sum(sums.astype(F32), 0, keepdims=True)

    grad_nope = grad_nope.transpose(2, 0, 1, 3).reshape(tokens, heads, NOPE)
    return grad_nope, grad_rope, grad_latent, owned


def solution(mesh):
    return jax.shard_map(
        local,
        mesh=mesh,
        in_specs=(
            P(AXES, None, None),
            P(AXES, None),
            P(AXES, None, None),
            P(AXES, None),
            P("dp", "seq", None),
            P("seq", None, None),
            P("seq", None, None),
            P(),
            P(),
            P(AXES, None),
        ),
        out_specs=(
            P(AXES, None, None),
            P(AXES, None),
            P(AXES, None),
            P("dp", "seq", None),
        ),
        check_vma=False,
    )
```

```python
import functools
import math

import jax
import jax.numpy as jnp
import numpy as np
from jax import lax
from jax.experimental import pallas as pl
from jax.experimental.pallas import tpu as pltpu
from jax.sharding import PartitionSpec as P

NOPE = 128
ROPE = 64
LATENT = 512
WIDTH = LATENT + ROPE
SCALE = (NOPE + ROPE) ** -0.5
LOG2E = math.log2(math.e)
MASKED = -1e30
AXES = ("dp", "seq")
NX, NY, NZ_HI, NZ_LO, NCORE = 4, 4, 2, 4, 2
NZ = NZ_HI * NZ_LO
PPS = 4
F32 = jnp.float32
BF16 = jnp.bfloat16


def place(i):
    x, z_lo = i % NX, i // NX % NZ_LO
    core, z_hi, y = i // 16 % NCORE, i // 32 % NZ_HI, i // 64
    return x, y, z_hi * NZ_LO + z_lo, core


def number(x, y, z, core):
    x, y, z, core = x % NX, y % NY, z % NZ, core % NCORE
    return ((y * NZ_HI + z // NZ_LO) * NCORE + core) * 16 + z % NZ_LO * NX + x


def permute(array, move):
    pairs = []
    for i in range(NX * NY * NZ * NCORE):
        x, y, z, core = place(i)
        dx, dz, dc = move(core)
        pairs.append((i, number(x + dx, y, z + dz, core + dc)))
    return lax.ppermute(array, AXES, pairs)


def swap(array):
    return permute(array, lambda core: (0, 0, 1))


def first_ring(array, step):
    return permute(array, lambda core: (0, step, 0) if core else (step, 0, 0))


def second_ring(array, step):
    return permute(array, lambda core: (step, 0, 0) if core else (0, step, 0))


def nt(a, b):
    return lax.dot_general(a, b, (((1,), (1,)), ((), ())), preferred_element_type=F32)


def tn(a, b):
    return lax.dot_general(a, b, (((0,), (0,)), ((), ())), preferred_element_type=F32)


def nn(a, b):
    return jnp.dot(a, b, preferred_element_type=F32)


def attention_kernel(counts, first, last, pair_ref, prompt_of_ref, prompt_len_ref, *refs):
    sources = len(counts)
    source_refs, refs = refs[:sources], refs[sources:]
    q_refs, refs = refs[:PPS], refs[PPS:]
    g_refs, refs = refs[:PPS], refs[PPS:]
    rope_refs, refs = refs[:PPS], refs[PPS:]
    (prompt_ref, own_ref, own_bias_ref), refs = refs[:3], refs[3:]
    if not first:
        (lat_in, turn_in), refs = refs[:2], refs[4:]
    (first_out, second_out, nope_out, rope_out), refs = refs[:4], refs[4:]
    if last:
        (lat_ref, turn_ref), refs = refs[:2], refs[2:]
    else:
        lat_ref, turn_ref = first_out, second_out
    latent_ref, rot_ref, bias_ref, weights, nope_part, rope_part, sems, weight_sems = refs
    step = pl.program_id(0)
    steps = pl.num_programs(0)
    slot = lax.rem(step, 2)

    tokens, prompts = own_ref.shape[0], prompt_ref.shape[0]

    @pl.when(step == 0)
    def _():
        for begin, rows_ref in ((0, prompt_ref), (prompts, own_ref)):
            here = pl.ds(begin, rows_ref.shape[0])
            latent_ref[here, :] = rows_ref[:, :LATENT]
            rotary = rows_ref[:, LATENT:]
            rot_ref[here, :] = jnp.concatenate([rotary, rotary], 1)
        live = prompt_len_ref[prompt_of_ref[lax.axis_index("dp"), lax.axis_index("seq")]]
        row = lax.broadcasted_iota(jnp.int32, (prompts, 2 * tokens), 0)
        bias_ref[:prompts, :] = jnp.where(row < live, 0.0, MASKED).astype(F32)
        own_bias = own_bias_ref[...]
        bias_ref[prompts:, :] = jnp.concatenate([own_bias, own_bias], 1)
        if first:
            lat_ref[...] = jnp.zeros_like(lat_ref)
            turn_ref[...] = jnp.zeros_like(turn_ref)
        else:
            lat_ref[...] = lat_in[...]
            turn_ref[...] = turn_in[...]

    def fetch(at):
        begin = 0
        for k in range(sources):
            ahead, lane_of = begin // PPS, begin % PPS

            @pl.when(at == ahead)
            def _(k=k, lane_of=lane_of):
                here = weights.at[at % 2, pl.ds(lane_of, counts[k])]
                pltpu.make_async_copy(source_refs[k], here, weight_sems.at[at % 2]).start()

            begin += counts[k]

    @pl.when(step == 0)
    def _():
        fetch(step)

    @pl.when(step + 1 < steps)
    def _():
        fetch(step + 1)

    pltpu.make_async_copy(weights.at[slot], weights.at[slot], weight_sems.at[slot]).wait()

    def copies(at, where):
        out = []
        for p in range(PPS):
            pair = pair_ref[at * PPS + p]
            out.append(pltpu.make_async_copy(nope_part.at[where, p], nope_out.at[pair], sems.at[where, 0, p]))
            lanes = pl.ds(pl.multiple_of(pair * 2 * ROPE, 2 * ROPE), 2 * ROPE)
            out.append(pltpu.make_async_copy(rope_part.at[where, p], rope_out.at[:, lanes], sems.at[where, 1, p]))
        return out

    @pl.when(step >= 2)
    def _():
        for copy in copies(step - 2, slot):
            copy.wait()

    latent = latent_ref[...]
    rot = rot_ref[...]
    bias = bias_ref[...]
    lane = lax.broadcasted_iota(jnp.int32, (tokens, 2 * ROPE), 1) // ROPE
    mine = lane == 0
    none = jnp.zeros((tokens, NOPE), BF16)
    zero = jnp.zeros((tokens, 2 * ROPE), BF16)
    kept = [{} for _ in range(PPS)]

    def project(p):
        up = nt(latent, weights[slot, p].reshape(4 * NOPE, LATENT)).astype(BF16)
        kept[p]["keys"] = jnp.concatenate([up[:, :256], rot], 1)
        kept[p]["values"] = up[:, 256:]

    def compare(p):
        q0, q1 = q_refs[p][0, 0], q_refs[p][0, 1]
        g0, g1 = g_refs[p][0, 0], g_refs[p][0, 1]
        rope = rope_refs[p][...]
        rope0, rope1 = jnp.where(mine, rope, zero), jnp.where(mine, zero, rope)
        kept[p]["queries"] = jnp.concatenate(
            [jnp.concatenate([q0, none, rope0], 1), jnp.concatenate([none, q1, rope1], 1)], 0
        )
        kept[p]["out_grad"] = jnp.concatenate(
            [jnp.concatenate([g0, none], 1), jnp.concatenate([none, g1], 1)], 0
        )
        keys = kept[p]["keys"]
        score0 = nt(jnp.concatenate([keys[:, :128], rot], 1), jnp.concatenate([q0, rope0], 1))
        score1 = nt(keys[:, 128:], jnp.concatenate([q1, rope1], 1))
        kept[p]["score"] = jnp.concatenate([score0, score1], 1)
        kept[p]["dprob"] = nt(kept[p]["values"], kept[p]["out_grad"])

    def soften(p):
        score = kept[p]["score"] * (SCALE * LOG2E) + bias
        dprob = kept[p]["dprob"]
        top = jnp.max(score, 0, keepdims=True)
        e = jnp.exp2(score - top)
        inverse = 1.0 / jnp.sum(e, 0, keepdims=True)
        delta = jnp.sum(e * dprob, 0, keepdims=True) * inverse
        prob = e * inverse
        kept[p]["prob"] = prob.astype(BF16)
        kept[p]["dscore"] = (prob * (dprob - delta) * SCALE).astype(BF16)

    def derive(p):
        keys, dscore = kept[p]["keys"], kept[p]["dscore"]
        dkeys = nn(dscore, kept[p]["queries"])
        dvalues = nn(kept[p]["prob"], kept[p]["out_grad"])
        kept[p]["turn"] = dkeys[:, 256:]
        kept[p]["grads"] = [dkeys[:, :256].astype(BF16), dvalues.astype(BF16)]
        dq0 = tn(dscore[:, :tokens], jnp.concatenate([keys[:, :128], rot], 1))
        dq1 = tn(dscore[:, tokens:], jnp.concatenate([keys[:, 128:256], rot], 1))
        nope_part[slot, p, 0] = dq0[:, :128].astype(BF16)
        nope_part[slot, p, 1] = dq1[:, :128].astype(BF16)
        rope_part[slot, p] = jnp.where(mine, dq0[:, 128:], dq1[:, 128:]).astype(BF16)

    stages = (project, compare, soften, derive)
    for tick in range(PPS + len(stages) - 1):
        for k in range(len(stages)):
            if 0 <= tick - k < PPS:
                stages[k](tick - k)
    turn_ref[...] += sum(kept[p]["turn"] for p in range(PPS))
    lat_ref[...] += nn(jnp.concatenate(sum([kept[p]["grads"] for p in range(PPS)], []), 1), weights[slot].reshape(PPS * 4 * NOPE, LATENT))

    for copy in copies(step, slot):
        copy.start()

    if last:

        @pl.when(step == steps - 1)
        def _():
            prompts = first_out.shape[0]
            turned = turn_ref[:, :ROPE] + turn_ref[:, ROPE:]
            total = jnp.concatenate([lat_ref[...], turned], 1)
            first_out[...] = total[:prompts]
            second_out[...] = total[prompts:].astype(BF16)

    @pl.when(step == steps - 1)
    def _():
        if total_steps(counts) > 1:
            for copy in copies(step - 1, 1 - slot):
                copy.wait()
        for copy in copies(step, slot):
            copy.wait()


def total_steps(counts):
    return sum(counts) // PPS


def attention(sources, scalars, q, g, rope, prompt, own, own_bias, state, last=False):
    counts = tuple(source.shape[0] for source in sources)
    first = state is None
    steps = total_steps(counts)
    tokens = own.shape[0]
    keys = prompt.shape[0] + tokens
    any_spec = pl.BlockSpec(memory_space=pl.ANY)

    head_specs = [
        pl.BlockSpec((1, 2, tokens, NOPE), lambda i, pair, *_, p=p: (pair[i * PPS + p], 0, 0, 0))
        for p in range(PPS)
    ]
    rope_specs = [
        pl.BlockSpec((tokens, 2 * ROPE), lambda i, pair, *_, p=p: (0, pair[i * PPS + p])) for p in range(PPS)
    ]

    def whole(shape):
        return pl.BlockSpec(shape, lambda i, *_: (0,) * len(shape))

    in_specs = [any_spec] * len(sources) + head_specs * 2 + rope_specs
    in_specs += [whole(prompt.shape), whole(own.shape), whole(own_bias.shape)]
    operands = list(sources)
    operands += [q] * PPS + [g] * PPS + [rope] * PPS + [prompt, own, own_bias]
    aliases = {}
    if not first:
        operands += list(state)
        in_specs += [whole((keys, LATENT)), whole((keys, 2 * ROPE)), any_spec, any_spec]
        aliases = {len(scalars) + len(operands) - 2: 2, len(scalars) + len(operands) - 1: 3}
    sums = (jax.ShapeDtypeStruct((keys, LATENT), F32), jax.ShapeDtypeStruct((keys, 2 * ROPE), F32))
    sum_scratch = []
    if last:
        sum_scratch = [pltpu.VMEM(s.shape, F32) for s in sums]
        sums = (jax.ShapeDtypeStruct((keys - tokens, WIDTH), F32), jax.ShapeDtypeStruct((tokens, WIDTH), BF16))
    return pl.pallas_call(
        functools.partial(attention_kernel, counts, first, last),
        out_shape=(
            *sums,
            jax.ShapeDtypeStruct(q.shape, BF16),
            jax.ShapeDtypeStruct(rope.shape, BF16),
        ),
        grid_spec=pltpu.PrefetchScalarGridSpec(
            num_scalar_prefetch=len(scalars),
            grid=(steps,),
            in_specs=in_specs,
            out_specs=(whole(sums[0].shape), whole(sums[1].shape), any_spec, any_spec),
            scratch_shapes=sum_scratch
            + [
                pltpu.VMEM((keys, LATENT), BF16),
                pltpu.VMEM((keys, 2 * ROPE), BF16),
                pltpu.VMEM((keys, 2 * tokens), F32),
                pltpu.VMEM((2, PPS, 2, 2, NOPE, LATENT), BF16),
                pltpu.VMEM((2, PPS, 2, tokens, NOPE), BF16),
                pltpu.VMEM((2, PPS, tokens, 2 * ROPE), BF16),
                pltpu.SemaphoreType.DMA((2, 2, PPS)),
                pltpu.SemaphoreType.DMA((2,)),
            ],
        ),
        input_output_aliases=aliases,
        compiler_params=pltpu.CompilerParams(vmem_limit_bytes=48 * 1024 * 1024),
        name="attention",
    )(*scalars, *operands)


def small_call(kernel, prompt_of, rows, dtype, scratch, name):
    block = pl.BlockSpec(rows.shape, lambda i, *_: (0, 0, 0))
    return pl.pallas_call(
        kernel,
        out_shape=jax.ShapeDtypeStruct(rows.shape, dtype),
        grid_spec=pltpu.PrefetchScalarGridSpec(
            num_scalar_prefetch=1, grid=(1,), in_specs=[block], out_specs=block, scratch_shapes=scratch
        ),
        name=name,
    )(prompt_of, rows)


def select_kernel(prompt_ref, rows_ref, out_ref):
    group = lax.axis_index("dp")
    for m in range(rows_ref.shape[0]):
        out_ref[m] = rows_ref[prompt_ref[group, m]]


def select(prompt_of, rows):
    return small_call(select_kernel, prompt_of, rows, rows.dtype, [], "select")


def collect_kernel(prompt_ref, parts_ref, out_ref, sums):
    group = lax.axis_index("dp")
    sums[...] = jnp.zeros_like(sums)
    for m in range(parts_ref.shape[0]):
        sums[prompt_ref[group, m]] += parts_ref[m]
    out_ref[...] = sums[...].astype(out_ref.dtype)


def collect(prompt_of, parts):
    return small_call(collect_kernel, prompt_of, parts, BF16, [pltpu.VMEM(parts.shape, F32)], "collect")


def local(
    query_nope,
    query_rope,
    out_grad,
    latent_rows,
    prompt_latent,
    key_weight,
    value_weight,
    prompt_of,
    prompt_len,
    response_ids,
):
    dp, seq = lax.axis_index("dp"), lax.axis_index("seq")
    members = lax.axis_size("seq")
    core = dp % NCORE
    z_lo, x = seq // NX, seq % NX
    tokens, heads = query_nope.shape[:2]
    rows = prompt_latent.shape[1]
    prompts = members * rows

    with jax.named_scope("weights_first_ring"):
        both = jnp.stack([key_weight.reshape(2, 2, NOPE, LATENT), value_weight.reshape(2, 2, NOPE, LATENT)], 1)
        here = lax.dynamic_index_in_dim(both, core, 0, keepdims=False)
        before, after = first_ring(here, 1), first_ring(here, -1)
        opposite = jnp.stack([first_ring(here[0], 2), first_ring(here[1], -2)])

    with jax.named_scope("prompt_gather"):
        copies = jnp.broadcast_to(prompt_latent, (members, rows, WIDTH))
        column = lax.all_to_all(copies, "dp", 0, 0, tiled=True)

    with jax.named_scope("weights_second_ring"):
        low, high = jnp.stack([here, before]), jnp.stack([after, opposite])
        low, high, column = lax.optimization_barrier((low, high, column))
        lead = [second_ring(low, 1), second_ring(high, -1)]
        near_peer = [swap(low), swap(high)]

    with jax.named_scope("prompt_exchange"):
        chosen = select(prompt_of, column)
        chosen, query_nope, out_grad = lax.optimization_barrier((chosen, query_nope, out_grad))
        prompt_rows = lax.all_to_all(chosen, "seq", 0, 0, tiled=True).reshape(prompts, WIDTH)

    with jax.named_scope("pair_numbers"):
        order = (0, -1, 1, 2)

        def numbers(side, *blocks):
            table = np.array([(a, far) for far, nears in blocks for a in nears], np.int32)
            kind = core ^ side
            dx = jnp.where(kind == 0, table[:, 0], table[:, 1])
            dz = jnp.where(kind == 0, table[:, 1], table[:, 0])
            return (((z_lo + dz) & 3) * NX + ((x + dx) & 3)) * 2 + kind

        near_pairs = jnp.concatenate([numbers(side, (0, order)) for side in range(2)])
        lead_pairs = jnp.concatenate([numbers(side, (-1, order[:2]), (1, order[2:])) for side in range(2)])
        rest_blocks = (-1, order[2:]), (1, order[:2]), (2, order[:2]), (2, order[2:])
        rest_pairs = [numbers(side, *rest_blocks) for side in range(2)]

    q = query_nope.reshape(tokens, heads // 2, 2, NOPE).transpose(1, 2, 0, 3)
    g = out_grad.reshape(tokens, heads // 2, 2, NOPE).transpose(1, 2, 0, 3)
    ids = response_ids[0]
    t = jnp.arange(tokens)
    own_ok = (t[:, None] <= t[None, :]) & (ids[:, None] == ids[None, :])
    own_bias = jnp.where(own_ok, 0.0, MASKED).astype(F32)

    def work(sources, pairs, state, last=False):
        scalars = (pairs, prompt_of, prompt_len)
        return attention(sources, scalars, q, g, query_rope, prompt_rows, latent_rows, own_bias, state, last)

    with jax.named_scope("weights_rest"):
        q, g, own_bias, low, high, *lead, prompt_rows = lax.optimization_barrier(
            (q, g, own_bias, low, high, *lead, prompt_rows)
        )
        rest = [second_ring(high, 1), second_ring(low, -1), second_ring(lead[0], 1), second_ring(lead[1], -1)]
        lead_peer = [swap(w) for w in lead]
    state = work([low, high, *near_peer], near_pairs, None)
    state = work([*lead, *lead_peer], lead_pairs, state)
    *rest, turn = lax.optimization_barrier((*rest, state[1]))
    state = (state[0], turn, *state[2:])
    rest_peer = [swap(w) for w in rest]
    state = work(rest, rest_pairs[0], state)
    prompt_part, grad_latent, grad_nope, grad_rope = work(rest_peer, rest_pairs[1], state, last=True)

    with jax.named_scope("prompt_return"):
        parts = lax.all_to_all(prompt_part.reshape(members, rows, WIDTH), "seq", 0, 0, tiled=True)
        sums = lax.all_to_all(collect(prompt_of, parts), "dp", 0, 0, tiled=True)
        owned = jnp.sum(sums.astype(F32), 0, keepdims=True)

    grad_nope = grad_nope.transpose(2, 0, 1, 3).reshape(tokens, heads, NOPE)
    return grad_nope, grad_rope, grad_latent, owned


def solution(mesh):
    return jax.shard_map(
        local,
        mesh=mesh,
        in_specs=(
            P(AXES, None, None),
            P(AXES, None),
            P(AXES, None, None),
            P(AXES, None),
            P("dp", "seq", None),
            P("seq", None, None),
            P("seq", None, None),
            P(),
            P(),
            P(AXES, None),
        ),
        out_specs=(
            P(AXES, None, None),
            P(AXES, None),
            P(AXES, None),
            P("dp", "seq", None),
        ),
        check_vma=False,
    )
```
